32 devices in a mesh: row: 4 (over z), col: 8 (over y, x, core).
Axes of the slice: x: 2, y: 2, z: 4, core: 2. Of those that a mesh axis runs over, the one named last changes fastest.
Arguments:
- activations: bfloat16 [1024, 28672], P(('row', 'col')), may hold values from -6 to 6
- gradients: bfloat16 [1024, 8192], P(('row', 'col')), may hold values from -6 to 6
- act_basis: bfloat16 [28672, 28672], P('col', 'row'), may hold values from -0.03125 to 0.03125
- grad_basis: bfloat16 [8192, 8192], P('row', 'col'), may hold values from -0.0625 to 0.0625
Outputs:
- correction: float32 [28672, 8192], P('row', 'col')
The draws below stay inside these ranges and needn't reach their ends.
All inputs are finite; a program needn't handle non-finite values.
Results may differ from the reference program's by a relative error of at most 0.0041.
Values may be sent and summed in bfloat16 or wider, within the bound.
A program may use at most 192 MiB of HBM per device.

```python
import jax
import jax.numpy as jnp
from jax import lax

D = 8192
FF = 28672
SEQS = 2
LEN = 512
TOKENS = 1024


def level_of(key, shape, cuts, least, top_value):
    level = 1.0
    for position, blocks in cuts:
        heights = jax.random.uniform(jax.random.fold_in(jax.random.fold_in(key, 6), position), (blocks,), jnp.float32, least / len(cuts), top_value / len(cuts))
        level = level * jnp.repeat(jnp.exp(heights), shape[position] // blocks).reshape((-1,) + (1,) * (len(shape) - 1 - position))
    return level


def noise(rng, dims, spread, limit, shards=(), kind=jnp.bfloat16):
    gain = level_of(rng, dims, shards, -0.22, 0.18) if shards else 1.0
    values = jax.random.normal(rng, dims, jnp.float32) * spread * gain
    return jnp.minimum(jnp.maximum(values, -limit), limit).astype(kind)


def setup_inputs(seed: int = 0) -> dict:
    key_list = jax.random.split(jax.random.key(seed), 5)
    return {
        "activations": noise(key_list[0], (TOKENS, FF), 1.0, 6.0, ((0, 32),)),
        "gradients": noise(key_list[1], (TOKENS, D), 1.0, 6.0, ((0, 32),)),
        "act_basis": noise(key_list[2], (FF, FF), FF ** -0.5, 0.03125, ((0, 8), (1, 4))),
        "grad_basis": noise(key_list[3], (D, D), D ** -0.5, 0.0625, ((0, 4), (1, 8))),
    }


def reference(activations, gradients, act_basis, grad_basis):
    rot_grads = jnp.dot(gradients, grad_basis, preferred_element_type=jnp.float32).astype(jnp.bfloat16)
    blocks = act_basis.reshape(FF, 8, FF // 8).transpose(1, 0, 2)

    def one_block(columns):
        rot_acts = jnp.dot(activations, columns, preferred_element_type=jnp.float32).astype(jnp.bfloat16)
        total = jnp.zeros((FF // 8, D), jnp.float32)
        for seq in range(SEQS):
            left = rot_acts[seq * LEN:(seq + 1) * LEN]
            right = rot_grads[seq * LEN:(seq + 1) * LEN]
            grad_s = lax.dot_general(left, right, (((0,), (0,)), ((), ())), preferred_element_type=jnp.float32)
            total = total + grad_s * grad_s
        return total

    stacked = lax.map(one_block, blocks)
    return stacked.reshape(FF, D) * (1.0 / (SEQS * LEN))
```

```python
import functools

import jax
import jax.numpy as jnp
from jax import lax
from jax.experimental import pallas as pl
from jax.experimental.pallas import tpu as pltpu
from jax.sharding import PartitionSpec as P

SEQS = 2
LEN = 512
CHUNKS = 2


def pick(array, index, axis):
    return lax.dynamic_index_in_dim(array, index, axis, keepdims=False)


def sum_shares(partial, cols, stage):
    c = lax.axis_index("col")
    bits = cols.bit_length() - 1
    tokens, width = partial.shape[0], partial.shape[-1]

    def halve(value, held, bit, dtype):
        axis = len(held) - 1 - held.index(bit)
        mine = lax.rem(lax.div(c, 1 << bit), 2)
        sent = pick(value, 1 - mine, axis).astype(dtype)
        kept = pick(value, mine, axis)
        perm = [(i, i ^ (1 << bit)) for i in range(cols)]
        got = lax.ppermute(sent, "col", perm)
        return kept + got.astype(jnp.float32), [b for b in held if b != bit]

    held = list(range(bits))
    if stage == 0:
        value = partial.reshape((2,) * bits + (tokens // cols, width))
        return halve(value, held, 0, jnp.float32)[0]
    value, held = partial, held[1:]
    half = width // 2
    parts = []
    for k, order in enumerate((held, held[::-1])):
        part, left = value[..., k * half : (k + 1) * half], list(held)
        for bit in order:
            part, left = halve(part, left, bit, jnp.bfloat16)
        parts.append(part)
    return jnp.concatenate([p.astype(jnp.bfloat16) for p in parts], axis=-1)


def gather_shares(value, cols):
    c = lax.axis_index("col")
    bits = cols.bit_length() - 1

    def double(part, bit):
        perm = [(i, i ^ (1 << bit)) for i in range(cols)]
        got = lax.ppermute(part, "col", perm)
        upper = lax.rem(lax.div(c, 1 << bit), 2) == 1
        return jnp.stack([jnp.where(upper, got, part), jnp.where(upper, part, got)])

    value = double(value, 0)
    rest = list(range(1, bits))
    half = value.shape[-1] // 2
    parts = []
    for k, order in enumerate((rest, rest[::-1])):
        part = value[..., k * half : (k + 1) * half]
        for bit in order:
            part = double(part, bit)
        axes = [order[::-1].index(bit) for bit in rest[::-1]]
        axes += list(range(len(axes), part.ndim))
        parts.append(part.transpose(axes))
    return jnp.concatenate(parts, axis=-1).reshape((cols,) + value.shape[1:])


def correction_tile(chunks, *refs):
    lefts, right, out = refs[:chunks], refs[chunks], refs[chunks + 1]
    rows, share, width = lefts[0].shape
    per_seq = rows // SEQS
    total = None
    for seq in range(SEQS):
        grad_s = None
        for k in range(chunks):
            left = lefts[k][seq * per_seq : (seq + 1) * per_seq].reshape(per_seq * share, width)
            term = lax.dot_general(
                left, right[k, seq], (((0,), (0,)), ((), ())), preferred_element_type=jnp.float32
            )
            grad_s = term if grad_s is None else grad_s + term
        total = grad_s * grad_s if total is None else total + grad_s * grad_s
    out[...] = total * (1.0 / (SEQS * LEN))


def correct(lefts, right):
    rows, share, height = lefts[0].shape
    tile = next(t for t in (512, 256, 128) if height % t == 0)
    width = right.shape[-1]
    return pl.pallas_call(
        functools.partial(correction_tile, len(lefts)),
        grid=(height // tile,),
        in_specs=[pl.BlockSpec((rows, share, tile), lambda i: (0, 0, i)) for _ in lefts]
        + [pl.BlockSpec(right.shape, lambda i: (0, 0, 0, 0))],
        out_specs=pl.BlockSpec((tile, width), lambda i: (i, 0)),
        out_shape=jax.ShapeDtypeStruct((height, width), jnp.float32),
        compiler_params=pltpu.CompilerParams(vmem_limit_bytes=40 << 20),
    )(*lefts, right)


def on_device(rows, cols, activations, gradients, act_basis, grad_basis):
    r = lax.axis_index("row")

    local_acts = lax.all_to_all(activations, "col", split_axis=1, concat_axis=0, tiled=True)
    tokens = local_acts.shape[0]
    share = tokens // CHUNKS

    tokens_here = gradients.shape[0]
    features = gradients.shape[1] // rows
    cut = lax.all_to_all(
        gradients.reshape(tokens_here, rows, features), "row", split_axis=1, concat_axis=0, tiled=True
    ).reshape(rows, tokens_here, features)
    whole_grads = gather_shares(cut, cols).transpose(1, 0, 2, 3).reshape(rows * tokens, features)

    chunks = [
        lax.all_gather(local_acts[k * share : (k + 1) * share], "row", axis=0, tiled=True)
        for k in range(CHUNKS)
    ]
    chunks[0], whole_grads = lax.optimization_barrier((chunks[0], whole_grads))
    paired = []
    for k in range(CHUNKS):
        if k == CHUNKS - 1:
            partial_grads = jnp.dot(whole_grads, grad_basis, preferred_element_type=jnp.float32)
            partial_grads, chunks[k] = lax.optimization_barrier((partial_grads, chunks[k]))
        partial = jnp.dot(chunks[k], act_basis, preferred_element_type=jnp.float32)
        if k == 0:
            whole_grads, partial = lax.optimization_barrier((whole_grads, partial))
        paired.append(sum_shares(partial, cols, 0))

    partial_grads = partial_grads.reshape(rows, tokens, -1)
    perms = [[(i, (i + shift) % rows) for i in range(rows)] for shift in range(rows)]
    summed = pick(partial_grads, r, 0)
    for shift in range(1, rows):
        sent = pick(partial_grads, lax.rem(r + shift, rows), 0).astype(jnp.bfloat16)
        summed = summed + lax.ppermute(sent, "row", perms[shift]).astype(jnp.float32)
    mine = summed.astype(jnp.bfloat16)

    rotated = []
    for k in range(CHUNKS):
        shares = sum_shares(paired[k], cols, 1)
        if k > 0:
            shares, rotated[k - 1], mine = lax.optimization_barrier((shares, rotated[k - 1], mine))
        whole = lax.all_gather(shares, "col", axis=0, tiled=True)
        rotated.append(whole.reshape(rows, share, -1))

    held = jnp.stack([mine] + [lax.ppermute(mine, "row", perms[shift]) for shift in range(1, rows)])
    rot_grads = jnp.stack([pick(held, lax.rem(r - b + rows, rows), 0) for b in range(rows)])

    per_seq = rows // SEQS
    right = (
        rot_grads.reshape(SEQS, per_seq, CHUNKS, share, -1)
        .transpose(2, 0, 1, 3, 4)
        .reshape(CHUNKS, SEQS, per_seq * share, -1)
    )
    return correct(rotated, right)


def solution(mesh):
    return jax.shard_map(
        functools.partial(on_device, mesh.shape["row"], mesh.shape["col"]),
        mesh=mesh,
        in_specs=(
            P(("row", "col"), None),
            P(("row", "col"), None),
            P("col", "row"),
            P("row", "col"),
        ),
        out_specs=P("row", "col"),
        check_vma=False,
    )
```
